32 devices in a mesh: groups: 2 (over y), rows: 4 (over z), chan: 4 (over x, core).
Axes of the slice: x: 2, y: 2, z: 4, core: 2. Of those that a mesh axis runs over, the one named last changes fastest.
Arguments:
- pair_act: bfloat16 [512, 256, 128], P(('groups', 'chan'), 'rows'), parts along dimension 0, may hold values from -6 to 6
- pair_mask: int32 [512, 256], P(('groups', 'chan'), 'rows'), parts along dimension 0, may hold values 0 or 1
- input_gain: float32 [2, 128], replicated, may hold values from 0.5 to 1.5
- input_bias: float32 [2, 128], replicated, may hold values from -3 to 3
- proj_weight: bfloat16 [2, 128, 4, 128], replicated, may hold values from -0.5 to 0.5
- gate_weight: bfloat16 [2, 128, 128], replicated, may hold values from -0.5 to 0.5
- output_gain: float32 [2, 128], replicated, may hold values from 0.5 to 1.5
- output_bias: float32 [2, 128], replicated, may hold values from -3 to 3
- out_weight: bfloat16 [2, 128, 128], replicated, may hold values from -0.5 to 0.5
Outputs:
- pair_out: bfloat16 [512, 256, 128], P(('groups', 'chan'), 'rows'), parts along dimension 0
The draws below stay inside these ranges and needn't reach their ends.
There are 2 independent parts, one for each index of `groups`. The reference program is written for one: setup_inputs(seed, part) draws one part's arguments, and reference() takes and returns one part's arrays. A program takes and returns all parts, laid end to end along the dimension named above; an argument that names none is the same for every part. Nothing has to cross between parts.
All inputs are finite; a program needn't handle non-finite values. No bound on the sum of `pair_mask` on one device may be relied on, other than what follows from the above.
Results may differ from the reference program's by a relative error of at most 0.0075.
Values may be sent and summed in bfloat16 or wider, within the bound.
A program may use at most 64 MiB of HBM per device.

```python
import jax
import jax.numpy as jnp
from jax import lax

PAIR_C = 128
TRI_C = 128
TOKENS = 256


def with_ends(drawn, rng, smallest, largest):
    place = [jax.random.randint(jax.random.fold_in(rng, axis), (), 0, length) for axis, length in enumerate(drawn.shape)]
    longest = drawn.shape.index(max(drawn.shape))
    beside = place[:longest] + [(place[longest] + 1) % drawn.shape[longest]] + place[longest + 1:]
    return drawn.at[tuple(place)].set(smallest).at[tuple(beside)].set(largest)


def block_scale(own_key, shape, cuts, least, largest):
    level = 1.0
    for position, blocks in cuts:
        heights = jax.random.uniform(jax.random.fold_in(jax.random.fold_in(own_key, 6), position), (blocks,), jnp.float32, least / len(cuts), largest / len(cuts))
        level = level * jnp.repeat(jnp.exp(heights), shape[position] // blocks).reshape((-1,) + (1,) * (len(shape) - 1 - position))
    return level


def centred(rng, shape, width, reach, pieces=(), kind=jnp.bfloat16):
    result = jax.random.normal(rng, shape, jnp.float32) * width
    if len(pieces) > 0:
        result = block_scale(rng, shape, pieces, -0.22, 0.18) * result
    return jnp.clip(result, min=-reach, max=reach).astype(kind)


def setup_inputs(seed: int = 0, part: int = 0) -> dict:
    key_list = jax.random.split(jax.random.key(seed), 10)
    part_splits = jax.random.split(jax.random.fold_in(key_list[9], part), 10)
    pair_act = centred(part_splits[0], (TOKENS, TOKENS, PAIR_C), 1.0, 6.0, ((0, 4), (1, 4)))
    pair_mask = with_ends((jax.random.randint(part_splits[1], (TOKENS, TOKENS), 0, 8) < 7).astype(jnp.int32), jax.random.fold_in(part_splits[1], 1), 0, 1)
    input_gain = jnp.clip(1.0 + 0.1 * jax.random.normal(key_list[2], (2, PAIR_C), jnp.float32), 0.5, 1.5)
    input_bias = centred(key_list[3], (2, PAIR_C), 0.5, 3.0, (), jnp.float32)
    proj_weight = centred(key_list[4], (2, PAIR_C, 4, TRI_C), PAIR_C ** -0.5, 0.5)
    gate_weight = centred(key_list[5], (2, PAIR_C, PAIR_C), PAIR_C ** -0.5, 0.5)
    output_gain = jnp.clip(1.0 + 0.1 * jax.random.normal(key_list[6], (2, TRI_C), jnp.float32), 0.5, 1.5)
    output_bias = centred(key_list[7], (2, TRI_C), 0.5, 3.0, (), jnp.float32)
    out_weight = centred(key_list[8], (2, TRI_C, PAIR_C), TRI_C ** -0.5, 0.5)
    return dict(pair_act=pair_act, pair_mask=pair_mask, input_gain=input_gain, input_bias=input_bias, proj_weight=proj_weight, gate_weight=gate_weight, output_gain=output_gain, output_bias=output_bias, out_weight=out_weight)


def layer_norm(values, norm_gain, norm_bias):
    center = values - lax.optimization_barrier(jnp.mean(values, axis=-1, keepdims=True))
    spread = lax.optimization_barrier(jnp.mean(center * center, axis=-1, keepdims=True))
    return center * lax.rsqrt(spread + 1e-05) * norm_gain + norm_bias

def tri_update(pair_now, mask_float, layer_index, incoming, input_gain, input_bias, proj_weight, gate_weight, output_gain, output_bias, out_weight):
    pair_width = pair_now.shape[-1]
    hidden_width = proj_weight.shape[-1]
    normed_in = layer_norm(pair_now.astype(jnp.float32), input_gain[layer_index], input_bias[layer_index]).astype(jnp.bfloat16)
    flat_in = normed_in.reshape(-1, pair_width)
    projected = jnp.dot(flat_in, proj_weight[layer_index].reshape(pair_width, 4 * hidden_width), preferred_element_type=jnp.float32)
    projected = projected.reshape(TOKENS, TOKENS, 4, hidden_width)
    left_edge = (jax.nn.sigmoid(projected[:, :, 1]) * projected[:, :, 0] * mask_float[:, :, None]).astype(jnp.bfloat16)
    right_edge = (jax.nn.sigmoid(projected[:, :, 3]) * projected[:, :, 2] * mask_float[:, :, None]).astype(jnp.bfloat16)
    gating = jax.nn.sigmoid(jnp.dot(flat_in, gate_weight[layer_index], preferred_element_type=jnp.float32)).reshape(TOKENS, TOKENS, pair_width)
    left_wide = left_edge.astype(jnp.float32)
    right_wide = right_edge.astype(jnp.float32)
    if incoming:
        combined = jnp.einsum('kic,kjc->ijc', left_wide, right_wide)
    else:
        combined = jnp.einsum('ikc,jkc->ijc', left_wide, right_wide)
    combined = lax.optimization_barrier(combined.astype(jnp.bfloat16))
    normed_out = layer_norm(combined.astype(jnp.float32), output_gain[layer_index], output_bias[layer_index]).astype(jnp.bfloat16)
    mixed_out = jnp.dot(normed_out.reshape(-1, hidden_width), out_weight[layer_index], preferred_element_type=jnp.float32)
    mixed_out = mixed_out.reshape(TOKENS, TOKENS, pair_width)
    return lax.optimization_barrier((pair_now.astype(jnp.float32) + gating * mixed_out).astype(jnp.bfloat16))

def reference(pair_act, pair_mask, input_gain, input_bias, proj_weight, gate_weight, output_gain, output_bias, out_weight):
    mask_float = pair_mask.astype(jnp.float32)
    after_out = tri_update(pair_act, mask_float, 0, False, input_gain, input_bias, proj_weight, gate_weight, output_gain, output_bias, out_weight)
    return tri_update(after_out, mask_float, 1, True, input_gain, input_bias, proj_weight, gate_weight, output_gain, output_bias, out_weight)
```

```python
import functools

import jax
import jax.numpy as jnp
from jax import lax
from jax.experimental import pallas as pl
from jax.experimental.pallas import tpu as pltpu
from jax.sharding import PartitionSpec as P


def layer_norm(values, norm_gain, norm_bias):
    center = values - jnp.mean(values, axis=-1, keepdims=True)
    spread = jnp.mean(center * center, axis=-1, keepdims=True)
    return center * lax.rsqrt(spread + 1e-05) * norm_gain + norm_bias


def outgoing_sum(left_split, right_split):
    return jnp.einsum(
        "cik,cjk->cij",
        left_split,
        lax.all_gather(right_split, "chan", axis=1, tiled=True),
        preferred_element_type=jnp.float32,
    )


def incoming_sum(left_split, right_split):
    summed = lax.psum_scatter(
        jnp.einsum(
            "cki,ckj->icj", left_split, right_split, preferred_element_type=jnp.float32
        ).astype(jnp.bfloat16),
        "chan",
        scatter_dimension=0,
        tiled=True,
    ).astype(jnp.float32)
    return jnp.transpose(summed, (1, 0, 2))


def output_mix(combined, layer_index, output_gain, output_bias, out_weight):
    pixels = lax.all_to_all(combined, "rows", split_axis=2, concat_axis=0, tiled=True)
    values = pixels.astype(jnp.float32)
    center = values - jnp.mean(values, axis=0, keepdims=True)
    spread = jnp.mean(center * center, axis=0, keepdims=True)
    normed_out = (
        center * lax.rsqrt(spread + 1e-05) * output_gain[layer_index][:, None, None]
        + output_bias[layer_index][:, None, None]
    ).astype(jnp.bfloat16)
    return jnp.einsum(
        "cij,cd->ijd", normed_out, out_weight[layer_index], preferred_element_type=jnp.float32
    )


def tri_layer(
    pair_now,
    mask_float,
    layer_index,
    incoming,
    input_gain,
    input_bias,
    proj_weight,
    gate_weight,
    output_gain,
    output_bias,
    out_weight,
):
    normed_in = layer_norm(
        pair_now.astype(jnp.float32), input_gain[layer_index], input_bias[layer_index]
    ).astype(jnp.bfloat16)
    projected = jnp.einsum(
        "ijd,dhc->hcij", normed_in, proj_weight[layer_index], preferred_element_type=jnp.float32
    )
    left_edge = (jax.nn.sigmoid(projected[1]) * projected[0] * mask_float[None]).astype(
        jnp.bfloat16
    )
    right_edge = (jax.nn.sigmoid(projected[3]) * projected[2] * mask_float[None]).astype(
        jnp.bfloat16
    )
    gating = jax.nn.sigmoid(
        jnp.einsum(
            "ijd,de->ije", normed_in, gate_weight[layer_index], preferred_element_type=jnp.float32
        )
    )
    left_split, right_split = (
        lax.all_to_all(left_edge, "rows", split_axis=0, concat_axis=2, tiled=True),
        lax.all_to_all(right_edge, "rows", split_axis=0, concat_axis=2, tiled=True),
    )
    if incoming:
        combined = incoming_sum(left_split, right_split)
    else:
        combined = outgoing_sum(left_split, right_split)
    combined = lax.optimization_barrier(combined.astype(jnp.bfloat16))
    mixed_out = output_mix(combined, layer_index, output_gain, output_bias, out_weight)
    return lax.optimization_barrier(
        (pair_now.astype(jnp.float32) + gating * mixed_out).astype(jnp.bfloat16)
    )


def on_device(
    pair_act,
    pair_mask,
    input_gain,
    input_bias,
    proj_weight,
    gate_weight,
    output_gain,
    output_bias,
    out_weight,
):
    mask_float = pair_mask.astype(jnp.float32)
    after_out = tri_layer(
        pair_act,
        mask_float,
        0,
        False,
        input_gain,
        input_bias,
        proj_weight,
        gate_weight,
        output_gain,
        output_bias,
        out_weight,
    )
    return tri_layer(
        after_out,
        mask_float,
        1,
        True,
        input_gain,
        input_bias,
        proj_weight,
        gate_weight,
        output_gain,
        output_bias,
        out_weight,
    )


def sigmoid(values):
    return 0.5 * jnp.tanh(0.5 * values) + 0.5


def swap_halves(low, high):
    half = low.shape[-1] // 2
    lane = lax.broadcasted_iota(jnp.int32, low.shape, low.ndim - 1)
    axis = low.ndim - 1
    first = jnp.where(lane < half, low, pltpu.roll(high, half, axis))
    second = jnp.where(lane < half, pltpu.roll(low, half, axis), high)
    return first, second


def fused_kernel(
    rows,
    chan,
    pair_ref,
    mask_ref,
    in_gain_ref,
    in_bias_ref,
    proj_ref,
    gate_w_ref,
    out_gain_ref,
    out_bias_ref,
    out_w_ref,
    out_ref,
    mid_ref,
    left_wide,
    right_wide,
    gate_buf,
    edge_send,
    edge_recv,
    sum_send,
    sum_recv,
    edge_ssem,
    edge_rsem,
    sum_ssem,
    sum_rsem,
):
    peers = rows * chan
    my_row = lax.axis_index("rows")
    my_chan = lax.axis_index("chan")
    me = my_chan * rows + my_row
    side = pair_ref.shape[1]
    width = pair_ref.shape[2]
    half = pair_ref.shape[0] // 2
    own = edge_send.shape[3]
    lanes = 2 * side

    def coords(peer):
        return {"rows": lax.rem(peer, rows), "chan": lax.div(peer, rows)}

    barrier = pltpu.get_barrier_semaphore()

    @pl.loop(1, peers)
    def _(step):
        peer = lax.rem(me + step, peers)
        pl.semaphore_signal(
            barrier, inc=1, device_id=coords(peer), device_id_type=pl.DeviceIdType.MESH
        )

    def edge_copy(u, step, peer):
        return pltpu.make_async_remote_copy(
            src_ref=edge_send.at[u, peer],
            dst_ref=edge_recv.at[u, me],
            send_sem=edge_ssem.at[u, step],
            recv_sem=edge_rsem.at[u, step],
            device_id=coords(peer),
            device_id_type=pl.DeviceIdType.MESH,
        )

    def sum_copy(u, step, peer):
        return pltpu.make_async_remote_copy(
            src_ref=sum_send.at[u, peer],
            dst_ref=sum_recv.at[u, me],
            send_sem=sum_ssem.at[u, step],
            recv_sem=sum_rsem.at[u, step],
            device_id=coords(peer),
            device_id_type=pl.DeviceIdType.MESH,
        )

    for u in range(2):
        source = pair_ref if u == 0 else mid_ref
        target = mid_ref if u == 0 else out_ref

        @pl.loop(0, half)
        def _(ip):
            cells = jnp.concatenate([source[ip], source[ip + half]], axis=0).astype(jnp.float32)
            center = cells - jnp.mean(cells, axis=-1, keepdims=True)
            spread = jnp.mean(center * center, axis=-1, keepdims=True)
            normed = (
                center * lax.rsqrt(spread + 1e-05) * in_gain_ref[u : u + 1, :]
                + in_bias_ref[u : u + 1, :]
            ).astype(jnp.bfloat16)
            projected = lax.dot_general(
                proj_ref[u], normed, (((1,), (1,)), ((), ())), preferred_element_type=jnp.float32
            )
            mask_row = mask_ref[pl.ds(ip, 1), :]
            left = sigmoid(projected[width : 2 * width]) * projected[:width] * mask_row
            right = sigmoid(projected[3 * width :]) * projected[2 * width : 3 * width] * mask_row
            left_wide[:, pl.ds(ip, 1), :] = left[:, None, :]
            right_wide[:, pl.ds(ip, 1), :] = right[:, None, :]
            gate_buf[ip] = sigmoid(
                jnp.dot(normed, gate_w_ref[u], preferred_element_type=jnp.float32)
            )

        if u == 0:
            pl.semaphore_wait(barrier, peers - 1)

        @pl.loop(1, peers)
        def _(step):
            peer = lax.rem(me + step, peers)
            edge_send[u, peer, 0] = left_wide[pl.ds(peer * own, own)].astype(jnp.bfloat16)
            edge_send[u, peer, 1] = right_wide[pl.ds(peer * own, own)].astype(jnp.bfloat16)
            edge_copy(u, step, peer).start()

        edge_recv[u, me, 0] = left_wide[pl.ds(me * own, own)].astype(jnp.bfloat16)
        edge_recv[u, me, 1] = right_wide[pl.ds(me * own, own)].astype(jnp.bfloat16)

        @pl.loop(1, peers)
        def _(step):
            edge_copy(u, step, lax.rem(me + step, peers)).wait()

        @pl.loop(0, own)
        def _(c):
            def whole(kind):
                pieces = []
                for a in range(chan):
                    first, second = [], []
                    for r in range(0, rows, 2):
                        low = edge_recv[u, a * rows + r, kind, c].astype(jnp.float32)
                        high = edge_recv[u, a * rows + r + 1, kind, c].astype(jnp.float32)
                        one, two = swap_halves(low, high)
                        first.append(one)
                        second.append(two)
                    pieces.append(jnp.concatenate(first, axis=1))
                    pieces.append(jnp.concatenate(second, axis=1))
                return jnp.concatenate(pieces, axis=0).astype(jnp.bfloat16)

            left = whole(0)
            right = whole(1)
            depth = 1 if u == 0 else 0
            summed = lax.dot_general(
                left,
                right,
                (((depth,), (depth,)), ((), ())),
                preferred_element_type=jnp.float32,
            )
            for a in range(chan):
                for r in range(0, rows, 2):
                    top = 2 * half * a
                    upper = summed[top : top + half, r * side : r * side + lanes]
                    lower = summed[top + half : top + 2 * half, r * side : r * side + lanes]
                    one, two = swap_halves(upper, lower)
                    sum_send[u, a * rows + r, c] = one.astype(jnp.bfloat16)
                    sum_send[u, a * rows + r + 1, c] = two.astype(jnp.bfloat16)

        @pl.loop(1, peers)
        def _(step):
            sum_copy(u, step, lax.rem(me + step, peers)).start()

        left_wide[pl.ds(me * own, own)] = sum_send[u, me].astype(jnp.float32)

        @pl.loop(1, peers)
        def _(step):
            sum_copy(u, step, lax.rem(me + step, peers)).wait()
            peer = lax.rem(me + peers - step, peers)
            left_wide[pl.ds(peer * own, own)] = sum_recv[u, peer].astype(jnp.float32)

        @pl.loop(0, half)
        def _(ip):
            values = left_wide[:, pl.ds(ip, 1), :].reshape(width, lanes)
            center = values - jnp.mean(values, axis=0, keepdims=True)
            spread = jnp.mean(center * center, axis=0, keepdims=True)
            normed = (
                center * lax.rsqrt(spread + 1e-05) * out_gain_ref[u] + out_bias_ref[u]
            ).astype(jnp.bfloat16)
            mixed = lax.dot_general(
                normed,
                out_w_ref[u],
                (((0,), (0,)), ((), ())),
                preferred_element_type=jnp.float32,
            )
            moved = gate_buf[ip] * mixed
            target[ip] = (source[ip].astype(jnp.float32) + moved[:side]).astype(jnp.bfloat16)
            target[ip + half] = (
                source[ip + half].astype(jnp.float32) + moved[side:]
            ).astype(jnp.bfloat16)


def fused_on_device(rows, chan):
    def run(
        pair_act,
        pair_mask,
        input_gain,
        input_bias,
        proj_weight,
        gate_weight,
        output_gain,
        output_bias,
        out_weight,
    ):
        first, side, width = pair_act.shape
        half = first // 2
        hidden = proj_weight.shape[-1]
        peers = rows * chan
        own = hidden // peers
        lanes = 2 * side
        mask_float = pair_mask.astype(jnp.float32)
        mask_rows = jnp.concatenate([mask_float[:half], mask_float[half:]], axis=1)
        proj_flat = jnp.transpose(proj_weight, (0, 2, 3, 1)).reshape(2, 4 * hidden, width)
        vmem = pl.BlockSpec(memory_space=pltpu.VMEM)
        return pl.pallas_call(
            functools.partial(fused_kernel, rows, chan),
            out_shape=jax.ShapeDtypeStruct(pair_act.shape, jnp.bfloat16),
            in_specs=[vmem] * 9,
            out_specs=vmem,
            scratch_shapes=[
                pltpu.VMEM((first, side, width), jnp.bfloat16),
                pltpu.VMEM((hidden, half, lanes), jnp.float32),
                pltpu.VMEM((hidden, half, lanes), jnp.float32),
                pltpu.VMEM((half, lanes, width), jnp.float32),
                pltpu.VMEM((2, peers, 2, own, half, lanes), jnp.bfloat16),
                pltpu.VMEM((2, peers, 2, own, half, lanes), jnp.bfloat16),
                pltpu.VMEM((2, peers, own, half, lanes), jnp.bfloat16),
                pltpu.VMEM((2, peers, own, half, lanes), jnp.bfloat16),
                pltpu.SemaphoreType.DMA((2, peers)),
                pltpu.SemaphoreType.DMA((2, peers)),
                pltpu.SemaphoreType.DMA((2, peers)),
                pltpu.SemaphoreType.DMA((2, peers)),
            ],
            compiler_params=pltpu.CompilerParams(
                collective_id=0, has_side_effects=True, vmem_limit_bytes=48 * 1024 * 1024
            ),
        )(
            pair_act,
            mask_rows,
            input_gain,
            input_bias,
            proj_flat,
            gate_weight,
            output_gain[:, :, None],
            output_bias[:, :, None],
            out_weight,
        )

    return run


def solution(mesh):
    in_specs = (
        P(("groups", "chan"), "rows", None),
        P(("groups", "chan"), "rows"),
        P(),
        P(),
        P(),
        P(),
        P(),
        P(),
        P(),
    )
    out_specs = P(("groups", "chan"), "rows", None)
    rows, chan = mesh.shape["rows"], mesh.shape["chan"]
    fused = fused_on_device(rows, chan)

    def choose(pair_act, pair_mask, *parameters):
        hidden = parameters[2].shape[-1]
        fits = (
            pair_act.shape[1] == 64
            and pair_act.shape[0] % 32 == 0
            and rows % 2 == 0
            and hidden % (rows * chan) == 0
        )
        body = fused if fits else on_device
        return body(pair_act, pair_mask, *parameters)

    return jax.shard_map(
        choose, mesh=mesh, in_specs=in_specs, out_specs=out_specs, check_vma=False
    )
```

```python
import functools

import jax
import jax.numpy as jnp
from jax import lax
from jax.experimental import pallas as pl
from jax.experimental.pallas import tpu as pltpu
from jax.sharding import PartitionSpec as P


def layer_norm(values, norm_gain, norm_bias):
    center = values - jnp.mean(values, axis=-1, keepdims=True)
    spread = jnp.mean(center * center, axis=-1, keepdims=True)
    return center * lax.rsqrt(spread + 1e-05) * norm_gain + norm_bias


def outgoing_sum(left_split, right_split):
    return jnp.einsum(
        "cik,cjk->cij",
        left_split,
        lax.all_gather(right_split, "chan", axis=1, tiled=True),
        preferred_element_type=jnp.float32,
    )


def incoming_sum(left_split, right_split):
    summed = lax.psum_scatter(
        jnp.einsum(
            "cki,ckj->icj", left_split, right_split, preferred_element_type=jnp.float32
        ).astype(jnp.bfloat16),
        "chan",
        scatter_dimension=0,
        tiled=True,
    ).astype(jnp.float32)
    return jnp.transpose(summed, (1, 0, 2))


def output_mix(combined, layer_index, output_gain, output_bias, out_weight):
    pixels = lax.all_to_all(combined, "rows", split_axis=2, concat_axis=0, tiled=True)
    values = pixels.astype(jnp.float32)
    center = values - jnp.mean(values, axis=0, keepdims=True)
    spread = jnp.mean(center * center, axis=0, keepdims=True)
    normed_out = (
        center * lax.rsqrt(spread + 1e-05) * output_gain[layer_index][:, None, None]
        + output_bias[layer_index][:, None, None]
    ).astype(jnp.bfloat16)
    return jnp.einsum(
        "cij,cd->ijd", normed_out, out_weight[layer_index], preferred_element_type=jnp.float32
    )


def tri_layer(
    pair_now,
    mask_float,
    layer_index,
    incoming,
    input_gain,
    input_bias,
    proj_weight,
    gate_weight,
    output_gain,
    output_bias,
    out_weight,
):
    normed_in = layer_norm(
        pair_now.astype(jnp.float32), input_gain[layer_index], input_bias[layer_index]
    ).astype(jnp.bfloat16)
    projected = jnp.einsum(
        "ijd,dhc->hcij", normed_in, proj_weight[layer_index], preferred_element_type=jnp.float32
    )
    left_edge = (jax.nn.sigmoid(projected[1]) * projected[0] * mask_float[None]).astype(
        jnp.bfloat16
    )
    right_edge = (jax.nn.sigmoid(projected[3]) * projected[2] * mask_float[None]).astype(
        jnp.bfloat16
    )
    gating = jax.nn.sigmoid(
        jnp.einsum(
            "ijd,de->ije", normed_in, gate_weight[layer_index], preferred_element_type=jnp.float32
        )
    )
    left_split, right_split = (
        lax.all_to_all(left_edge, "rows", split_axis=0, concat_axis=2, tiled=True),
        lax.all_to_all(right_edge, "rows", split_axis=0, concat_axis=2, tiled=True),
    )
    if incoming:
        combined = incoming_sum(left_split, right_split)
    else:
        combined = outgoing_sum(left_split, right_split)
    combined = lax.optimization_barrier(combined.astype(jnp.bfloat16))
    mixed_out = output_mix(combined, layer_index, output_gain, output_bias, out_weight)
    return lax.optimization_barrier(
        (pair_now.astype(jnp.float32) + gating * mixed_out).astype(jnp.bfloat16)
    )


def on_device(
    pair_act,
    pair_mask,
    input_gain,
    input_bias,
    proj_weight,
    gate_weight,
    output_gain,
    output_bias,
    out_weight,
):
    mask_float = pair_mask.astype(jnp.float32)
    after_out = tri_layer(
        pair_act,
        mask_float,
        0,
        False,
        input_gain,
        input_bias,
        proj_weight,
        gate_weight,
        output_gain,
        output_bias,
        out_weight,
    )
    return tri_layer(
        after_out,
        mask_float,
        1,
        True,
        input_gain,
        input_bias,
        proj_weight,
        gate_weight,
        output_gain,
        output_bias,
        out_weight,
    )


PARTS = 2
UNROLL = 4


def sigmoid(values):
    return 0.5 * jnp.tanh(0.5 * values) + 0.5


def swap_halves(low, high):
    half = low.shape[-1] // 2
    lane = lax.broadcasted_iota(jnp.int32, low.shape, low.ndim - 1)
    axis = low.ndim - 1
    first = jnp.where(lane < half, low, pltpu.roll(high, half, axis))
    second = jnp.where(lane < half, pltpu.roll(low, half, axis), high)
    return first, second


def fused_kernel(
    rows,
    chan,
    pair_ref,
    mask_ref,
    in_gain_ref,
    in_bias_ref,
    proj_ref,
    gate_w_ref,
    out_gain_ref,
    out_bias_ref,
    out_w_ref,
    out_ref,
    mid_ref,
    left_wide,
    right_wide,
    sum_wide,
    gate_buf,
    edge_send,
    edge_recv,
    sum_send,
    sum_recv,
    edge_ssem,
    edge_rsem,
    sum_ssem,
    sum_rsem,
):
    peers = rows * chan
    my_row = lax.axis_index("rows")
    my_chan = lax.axis_index("chan")
    me = my_chan * rows + my_row
    side = pair_ref.shape[1]
    width = pair_ref.shape[2]
    half = pair_ref.shape[0] // 2
    own = edge_send.shape[4]
    depth = half // PARTS
    lanes = 2 * side

    def coords(peer):
        return {"rows": lax.rem(peer, rows), "chan": lax.div(peer, rows)}

    barrier = pltpu.get_barrier_semaphore()

    @pl.loop(1, peers)
    def _(step):
        peer = lax.rem(me + step, peers)
        pl.semaphore_signal(
            barrier, inc=1, device_id=coords(peer), device_id_type=pl.DeviceIdType.MESH
        )

    def edge_copy(u, part, step, peer):
        return pltpu.make_async_remote_copy(
            src_ref=edge_send.at[u, part, peer],
            dst_ref=edge_recv.at[u, part, me],
            send_sem=edge_ssem.at[u, part, step],
            recv_sem=edge_rsem.at[u, part, step],
            device_id=coords(peer),
            device_id_type=pl.DeviceIdType.MESH,
        )

    def sum_copy(u, part, step, peer):
        return pltpu.make_async_remote_copy(
            src_ref=sum_send.at[u, part, peer],
            dst_ref=sum_recv.at[u, part, me],
            send_sem=sum_ssem.at[u, part, step],
            recv_sem=sum_rsem.at[u, part, step],
            device_id=coords(peer),
            device_id_type=pl.DeviceIdType.MESH,
        )

    def make_edges(u, part, source):
        @pl.loop(part * depth, (part + 1) * depth, unroll=UNROLL)
        def _(ip):
            cells = jnp.concatenate([source[ip], source[ip + half]], axis=0).astype(jnp.float32)
            center = cells - jnp.mean(cells, axis=-1, keepdims=True)
            spread = jnp.mean(center * center, axis=-1, keepdims=True)
            normed = (
                center * lax.rsqrt(spread + 1e-05) * in_gain_ref[u : u + 1, :]
                + in_bias_ref[u : u + 1, :]
            ).astype(jnp.bfloat16)
            projected = lax.dot_general(
                proj_ref[u], normed, (((1,), (1,)), ((), ())), preferred_element_type=jnp.float32
            )
            mask_row = mask_ref[pl.ds(ip, 1), :]
            left = sigmoid(projected[width : 2 * width]) * projected[:width] * mask_row
            right = sigmoid(projected[3 * width :]) * projected[2 * width : 3 * width] * mask_row
            left_wide[:, pl.ds(ip, 1), :] = left[:, None, :]
            right_wide[:, pl.ds(ip, 1), :] = right[:, None, :]
            gate_buf[u, ip] = sigmoid(
                jnp.dot(normed, gate_w_ref[u], preferred_element_type=jnp.float32)
            )

    def narrow(wide, part, peer):
        return wide[pl.ds(peer * own, own), part * depth : (part + 1) * depth, :].astype(
            jnp.bfloat16
        )

    def send_edges(u, part):
        @pl.loop(1, peers)
        def _(step):
            peer = lax.rem(me + step, peers)
            edge_send[u, part, peer, 0] = narrow(left_wide, part, peer)
            edge_send[u, part, peer, 1] = narrow(right_wide, part, peer)
            edge_copy(u, part, step, peer).start()

        edge_recv[u, part, me, 0] = narrow(left_wide, part, me)
        edge_recv[u, part, me, 1] = narrow(right_wide, part, me)

    def wait_edges(u, part):
        @pl.loop(1, peers)
        def _(step):
            edge_copy(u, part, step, lax.rem(me + step, peers)).wait()

    def make_sums(u):
        @pl.loop(0, own, unroll=2)
        def _(c):
            def whole(kind):
                pieces = []
                for a in range(chan):
                    first, second = [], []
                    for r in range(0, rows, 2):
                        low, high = (
                            jnp.concatenate(
                                [edge_recv[u, part, peer, kind, c] for part in range(PARTS)],
                                axis=0,
                            ).astype(jnp.float32)
                            for peer in (a * rows + r, a * rows + r + 1)
                        )
                        one, two = swap_halves(low, high)
                        first.append(one)
                        second.append(two)
                    pieces.append(jnp.concatenate(first, axis=1))
                    pieces.append(jnp.concatenate(second, axis=1))
                return jnp.concatenate(pieces, axis=0).astype(jnp.bfloat16)

            left = whole(0)
            right = whole(1)
            over = 1 if u == 0 else 0
            summed = lax.dot_general(
                left,
                right,
                (((over,), (over,)), ((), ())),
                preferred_element_type=jnp.float32,
            )
            for a in range(chan):
                for r in range(0, rows, 2):
                    top = 2 * half * a
                    upper = summed[top : top + half, r * side : r * side + lanes]
                    lower = summed[top + half : top + 2 * half, r * side : r * side + lanes]
                    one, two = swap_halves(upper, lower)
                    for part in range(PARTS):
                        piece = slice(part * depth, (part + 1) * depth)
                        sum_send[u, part, a * rows + r, c] = one[piece].astype(jnp.bfloat16)
                        sum_send[u, part, a * rows + r + 1, c] = two[piece].astype(jnp.bfloat16)

    def send_sums(u, part):
        @pl.loop(1, peers)
        def _(step):
            sum_copy(u, part, step, lax.rem(me + step, peers)).start()

    def take_sums(u, part):
        piece = slice(part * depth, (part + 1) * depth)
        sum_wide[pl.ds(me * own, own), piece, :] = sum_send[u, part, me].astype(jnp.float32)

        @pl.loop(1, peers)
        def _(step):
            sum_copy(u, part, step, lax.rem(me + step, peers)).wait()
            peer = lax.rem(me + peers - step, peers)
            sum_wide[pl.ds(peer * own, own), piece, :] = sum_recv[u, part, peer].astype(
                jnp.float32
            )

    def mix(u, part, source, target):
        @pl.loop(part * depth, (part + 1) * depth, unroll=UNROLL)
        def _(ip):
            values = sum_wide[:, pl.ds(ip, 1), :].reshape(width, lanes)
            center = values - jnp.mean(values, axis=0, keepdims=True)
            spread = jnp.mean(center * center, axis=0, keepdims=True)
            normed = (
                center * lax.rsqrt(spread + 1e-05) * out_gain_ref[u] + out_bias_ref[u]
            ).astype(jnp.bfloat16)
            mixed = lax.dot_general(
                normed,
                out_w_ref[u],
                (((0,), (0,)), ((), ())),
                preferred_element_type=jnp.float32,
            )
            moved = gate_buf[u, ip] * mixed
            target[ip] = (source[ip].astype(jnp.float32) + moved[:side]).astype(jnp.bfloat16)
            target[ip + half] = (
                source[ip + half].astype(jnp.float32) + moved[side:]
            ).astype(jnp.bfloat16)

    for part in range(PARTS):
        make_edges(0, part, pair_ref)
        if part == 0:
            pl.semaphore_wait(barrier, peers - 1)
        send_edges(0, part)
    for part in range(PARTS):
        wait_edges(0, part)
    make_sums(0)
    for part in range(PARTS):
        send_sums(0, part)
    for part in range(PARTS):
        take_sums(0, part)
        mix(0, part, pair_ref, mid_ref)
        make_edges(1, part, mid_ref)
        send_edges(1, part)
    for part in range(PARTS):
        wait_edges(1, part)
    make_sums(1)
    for part in range(PARTS):
        send_sums(1, part)
    for part in range(PARTS):
        take_sums(1, part)
        mix(1, part, mid_ref, out_ref)


def fused_on_device(rows, chan):
    def run(
        pair_act,
        pair_mask,
        input_gain,
        input_bias,
        proj_weight,
        gate_weight,
        output_gain,
        output_bias,
        out_weight,
    ):
        first, side, width = pair_act.shape
        half = first // 2
        hidden = proj_weight.shape[-1]
        peers = rows * chan
        own = hidden // peers
        lanes = 2 * side
        mask_float = pair_mask.astype(jnp.float32)
        mask_rows = jnp.concatenate([mask_float[:half], mask_float[half:]], axis=1)
        proj_flat = jnp.transpose(proj_weight, (0, 2, 3, 1)).reshape(2, 4 * hidden, width)
        vmem = pl.BlockSpec(memory_space=pltpu.VMEM)
        return pl.pallas_call(
            functools.partial(fused_kernel, rows, chan),
            out_shape=jax.ShapeDtypeStruct(pair_act.shape, jnp.bfloat16),
            in_specs=[vmem] * 9,
            out_specs=vmem,
            scratch_shapes=[
                pltpu.VMEM((first, side, width), jnp.bfloat16),
                pltpu.VMEM((hidden, half, lanes), jnp.float32),
                pltpu.VMEM((hidden, half, lanes), jnp.float32),
                pltpu.VMEM((hidden, half, lanes), jnp.float32),
                pltpu.VMEM((2, half, lanes, width), jnp.float32),
                pltpu.VMEM((2, PARTS, peers, 2, own, half // PARTS, lanes), jnp.bfloat16),
                pltpu.VMEM((2, PARTS, peers, 2, own, half // PARTS, lanes), jnp.bfloat16),
                pltpu.VMEM((2, PARTS, peers, own, half // PARTS, lanes), jnp.bfloat16),
                pltpu.VMEM((2, PARTS, peers, own, half // PARTS, lanes), jnp.bfloat16),
                pltpu.SemaphoreType.DMA((2, PARTS, peers)),
                pltpu.SemaphoreType.DMA((2, PARTS, peers)),
                pltpu.SemaphoreType.DMA((2, PARTS, peers)),
                pltpu.SemaphoreType.DMA((2, PARTS, peers)),
            ],
            compiler_params=pltpu.CompilerParams(
                collective_id=0, has_side_effects=True, vmem_limit_bytes=48 * 1024 * 1024
            ),
        )(
            pair_act,
            mask_rows,
            input_gain,
            input_bias,
            proj_flat,
            gate_weight,
            output_gain[:, :, None],
            output_bias[:, :, None],
            out_weight,
        )

    return run


def solution(mesh):
    in_specs = (
        P(("groups", "chan"), "rows", None),
        P(("groups", "chan"), "rows"),
        P(),
        P(),
        P(),
        P(),
        P(),
        P(),
        P(),
    )
    out_specs = P(("groups", "chan"), "rows", None)
    rows, chan = mesh.shape["rows"], mesh.shape["chan"]
    fused = fused_on_device(rows, chan)

    def choose(pair_act, pair_mask, *parameters):
        hidden = parameters[2].shape[-1]
        fits = (
            pair_act.shape[1] == 64
            and pair_act.shape[0] % (32 * PARTS) == 0
            and rows % 2 == 0
            and hidden % (rows * chan) == 0
        )
        body = fused if fits else on_device
        return body(pair_act, pair_mask, *parameters)

    return jax.shard_map(
        choose, mesh=mesh, in_specs=in_specs, out_specs=out_specs, check_vma=False
    )
```

```python
import functools

import jax
import jax.numpy as jnp
from jax import lax
from jax.experimental import pallas as pl
from jax.experimental.pallas import tpu as pltpu
from jax.sharding import PartitionSpec as P


def layer_norm(values, norm_gain, norm_bias):
    center = values - jnp.mean(values, axis=-1, keepdims=True)
    spread = jnp.mean(center * center, axis=-1, keepdims=True)
    return center * lax.rsqrt(spread + 1e-05) * norm_gain + norm_bias


def outgoing_sum(left_split, right_split):
    return jnp.einsum(
        "cik,cjk->cij",
        left_split,
        lax.all_gather(right_split, "chan", axis=1, tiled=True),
        preferred_element_type=jnp.float32,
    )


def incoming_sum(left_split, right_split):
    summed = lax.psum_scatter(
        jnp.einsum(
            "cki,ckj->icj", left_split, right_split, preferred_element_type=jnp.float32
        ).astype(jnp.bfloat16),
        "chan",
        scatter_dimension=0,
        tiled=True,
    ).astype(jnp.float32)
    return jnp.transpose(summed, (1, 0, 2))


def output_mix(combined, layer_index, output_gain, output_bias, out_weight):
    pixels = lax.all_to_all(combined, "rows", split_axis=2, concat_axis=0, tiled=True)
    values = pixels.astype(jnp.float32)
    center = values - jnp.mean(values, axis=0, keepdims=True)
    spread = jnp.mean(center * center, axis=0, keepdims=True)
    normed_out = (
        center * lax.rsqrt(spread + 1e-05) * output_gain[layer_index][:, None, None]
        + output_bias[layer_index][:, None, None]
    ).astype(jnp.bfloat16)
    return jnp.einsum(
        "cij,cd->ijd", normed_out, out_weight[layer_index], preferred_element_type=jnp.float32
    )


def tri_layer(
    pair_now,
    mask_float,
    layer_index,
    incoming,
    input_gain,
    input_bias,
    proj_weight,
    gate_weight,
    output_gain,
    output_bias,
    out_weight,
):
    normed_in = layer_norm(
        pair_now.astype(jnp.float32), input_gain[layer_index], input_bias[layer_index]
    ).astype(jnp.bfloat16)
    projected = jnp.einsum(
        "ijd,dhc->hcij", normed_in, proj_weight[layer_index], preferred_element_type=jnp.float32
    )
    left_edge = (jax.nn.sigmoid(projected[1]) * projected[0] * mask_float[None]).astype(
        jnp.bfloat16
    )
    right_edge = (jax.nn.sigmoid(projected[3]) * projected[2] * mask_float[None]).astype(
        jnp.bfloat16
    )
    gating = jax.nn.sigmoid(
        jnp.einsum(
            "ijd,de->ije", normed_in, gate_weight[layer_index], preferred_element_type=jnp.float32
        )
    )
    left_split, right_split = (
        lax.all_to_all(left_edge, "rows", split_axis=0, concat_axis=2, tiled=True),
        lax.all_to_all(right_edge, "rows", split_axis=0, concat_axis=2, tiled=True),
    )
    if incoming:
        combined = incoming_sum(left_split, right_split)
    else:
        combined = outgoing_sum(left_split, right_split)
    combined = lax.optimization_barrier(combined.astype(jnp.bfloat16))
    mixed_out = output_mix(combined, layer_index, output_gain, output_bias, out_weight)
    return lax.optimization_barrier(
        (pair_now.astype(jnp.float32) + gating * mixed_out).astype(jnp.bfloat16)
    )


def on_device(
    pair_act,
    pair_mask,
    input_gain,
    input_bias,
    proj_weight,
    gate_weight,
    output_gain,
    output_bias,
    out_weight,
):
    mask_float = pair_mask.astype(jnp.float32)
    after_out = tri_layer(
        pair_act,
        mask_float,
        0,
        False,
        input_gain,
        input_bias,
        proj_weight,
        gate_weight,
        output_gain,
        output_bias,
        out_weight,
    )
    return tri_layer(
        after_out,
        mask_float,
        1,
        True,
        input_gain,
        input_bias,
        proj_weight,
        gate_weight,
        output_gain,
        output_bias,
        out_weight,
    )


PARTS = 2
GROUPS = 2
UNROLL = 4


def sigmoid(values):
    return 0.5 * jnp.tanh(0.5 * values) + 0.5


def swap_halves(low, high):
    half = low.shape[-1] // 2
    lane = lax.broadcasted_iota(jnp.int32, low.shape, low.ndim - 1)
    axis = low.ndim - 1
    first = jnp.where(lane < half, low, pltpu.roll(high, half, axis))
    second = jnp.where(lane < half, pltpu.roll(low, half, axis), high)
    return first, second


def fused_kernel(
    rows,
    chan,
    pair_ref,
    mask_ref,
    in_gain_ref,
    in_bias_ref,
    proj_ref,
    gate_w_ref,
    out_gain_ref,
    out_bias_ref,
    out_w_ref,
    out_ref,
    mid_ref,
    left_wide,
    right_wide,
    sum_wide,
    gate_buf,
    left_send,
    right_send,
    left_recv,
    right_recv,
    sum_send,
    sum_recv,
    left_ssem,
    left_rsem,
    right_ssem,
    right_rsem,
    sum_ssem,
    sum_rsem,
):
    owners = 2 * chan
    peers = rows * chan
    my_row = lax.axis_index("rows")
    my_chan = lax.axis_index("chan")
    my_half = lax.div(my_row, 2)
    slot = my_chan * 2 + lax.rem(my_row, 2)
    me = my_half * owners + slot
    side = pair_ref.shape[1]
    width = pair_ref.shape[2]
    half = pair_ref.shape[0] // 2
    batch = left_send.shape[4]
    depth = half // PARTS
    lanes = 2 * side

    def coords(peer):
        place = lax.rem(peer, owners)
        return {
            "rows": 2 * lax.div(peer, owners) + lax.rem(place, 2),
            "chan": lax.div(place, 2),
        }

    barrier = pltpu.get_barrier_semaphore()

    @pl.loop(1, peers)
    def _(step):
        peer = lax.rem(me + step, peers)
        pl.semaphore_signal(
            barrier, inc=1, device_id=coords(peer), device_id_type=pl.DeviceIdType.MESH
        )

    def near(step):
        return lax.rem(slot + step, owners)

    def remote(src, dst, ssem, rsem, peer):
        return pltpu.make_async_remote_copy(
            src_ref=src,
            dst_ref=dst,
            send_sem=ssem,
            recv_sem=rsem,
            device_id=coords(peer),
            device_id_type=pl.DeviceIdType.MESH,
        )

    def left_copy(u, part, group, step):
        where = (u, part, group)
        if u == 0:
            place, mine = near(step), slot
            peer = my_half * owners + place
        else:
            peer, mine = lax.rem(me + step, peers), me
            place = lax.rem(peer, owners)
        return remote(
            left_send.at[(*where, place)],
            left_recv.at[(*where, mine)],
            left_ssem.at[(*where, step)],
            left_rsem.at[(*where, step)],
            peer,
        )

    def right_copy(u, part, group, step):
        where = (u, part, group)
        return remote(
            right_send.at[(*where, near(step))],
            right_recv.at[(*where, slot)],
            right_ssem.at[(*where, step)],
            right_rsem.at[(*where, step)],
            my_half * owners + near(step),
        )

    def sum_copy(u, part, group, step):
        where = (u, part, group)
        if u == 0:
            place, mine = lax.rem(me + step, peers), me
            peer = place
        else:
            place, mine = near(step), slot
            peer = my_half * owners + place
        return remote(
            sum_send.at[(*where, place)],
            sum_recv.at[(*where, mine)],
            sum_ssem.at[(*where, step)],
            sum_rsem.at[(*where, step)],
            peer,
        )

    def make_edges(u, part, source):
        @pl.loop(part * depth, (part + 1) * depth, unroll=UNROLL)
        def _(ip):
            cells = jnp.concatenate([source[ip], source[ip + half]], axis=0).astype(jnp.float32)
            center = cells - jnp.mean(cells, axis=-1, keepdims=True)
            spread = jnp.mean(center * center, axis=-1, keepdims=True)
            normed = (
                center * lax.rsqrt(spread + 1e-05) * in_gain_ref[u : u + 1, :]
                + in_bias_ref[u : u + 1, :]
            ).astype(jnp.bfloat16)
            projected = lax.dot_general(
                proj_ref[u], normed, (((1,), (1,)), ((), ())), preferred_element_type=jnp.float32
            )
            mask_row = mask_ref[pl.ds(ip, 1), :]
            left = sigmoid(projected[width : 2 * width]) * projected[:width] * mask_row
            right = sigmoid(projected[3 * width :]) * projected[2 * width : 3 * width] * mask_row
            left_wide[:, pl.ds(ip, 1), :] = left[:, None, :]
            right_wide[:, pl.ds(ip, 1), :] = right[:, None, :]
            gate_buf[u, ip] = sigmoid(
                jnp.dot(normed, gate_w_ref[u], preferred_element_type=jnp.float32)
            )

    def send_edges(u, part):
        piece = slice(part * depth, (part + 1) * depth)
        for group in range(GROUPS):

            @pl.loop(0, owners)
            def _(place):
                first = (place * GROUPS + group) * batch
                left_send[u, part, group, place] = left_wide[
                    pl.ds(first, batch), piece, :
                ].astype(jnp.bfloat16)
                right_send[u, part, group, place] = right_wide[
                    pl.ds(first, batch), piece, :
                ].astype(jnp.bfloat16)

            @pl.loop(1, owners)
            def _(step):
                right_copy(u, part, group, step).start()

            @pl.loop(1, owners if u == 0 else peers)
            def _(step):
                left_copy(u, part, group, step).start()

            right_recv[u, part, group, slot] = right_send[u, part, group, slot]
            left_recv[u, part, group, slot if u == 0 else me] = left_send[u, part, group, slot]

    def wait_edges(u, part, group):
        @pl.loop(1, owners)
        def _(step):
            right_copy(u, part, group, step).wait()

        @pl.loop(1, owners if u == 0 else peers)
        def _(step):
            left_copy(u, part, group, step).wait()

    def make_sums(u, group):
        @pl.loop(0, batch, unroll=2)
        def _(c):
            def whole(edges, first):
                pieces = []
                for a in range(chan):
                    low, high = (
                        jnp.concatenate(
                            [edges[u, part, group, place, c] for part in range(PARTS)], axis=0
                        ).astype(jnp.float32)
                        for place in (first + 2 * a, first + 2 * a + 1)
                    )
                    pieces.extend(swap_halves(low, high))
                return jnp.concatenate(pieces, axis=0).astype(jnp.bfloat16)

            if u == 0:
                left = whole(left_recv, 0)
            else:
                left = jnp.concatenate([whole(left_recv, 0), whole(left_recv, owners)], axis=1)
            right = whole(right_recv, 0)
            over = 1 if u == 0 else 0
            summed = lax.dot_general(
                left,
                right,
                (((over,), (over,)), ((), ())),
                preferred_element_type=jnp.float32,
            )
            for a in range(chan):
                for tile in range(summed.shape[1] // lanes):
                    top = 2 * half * a
                    columns = slice(tile * lanes, (tile + 1) * lanes)
                    one, two = swap_halves(
                        summed[top : top + half, columns],
                        summed[top + half : top + 2 * half, columns],
                    )
                    place = tile * owners + 2 * a
                    for part in range(PARTS):
                        piece = slice(part * depth, (part + 1) * depth)
                        sum_send[u, part, group, place, c] = one[piece].astype(jnp.bfloat16)
                        sum_send[u, part, group, place + 1, c] = two[piece].astype(jnp.bfloat16)

    def send_sums(u, part, group):
        @pl.loop(1, peers if u == 0 else owners)
        def _(step):
            sum_copy(u, part, group, step).start()

    def take_sums(u, part):
        piece = slice(part * depth, (part + 1) * depth)
        mine = me if u == 0 else slot
        for group in range(GROUPS):
            sum_recv[u, part, group, mine] = sum_send[u, part, group, mine]

            @pl.loop(1, peers if u == 0 else owners)
            def _(step):
                sum_copy(u, part, group, step).wait()

            @pl.loop(0, owners)
            def _(place):
                total = sum_recv[u, part, group, place].astype(jnp.float32)
                if u == 0:
                    total += sum_recv[u, part, group, place + owners].astype(jnp.float32)
                first = (place * GROUPS + group) * batch
                sum_wide[pl.ds(first, batch), piece, :] = total

    def mix(u, part, source, target):
        @pl.loop(part * depth, (part + 1) * depth, unroll=UNROLL)
        def _(ip):
            values = sum_wide[:, pl.ds(ip, 1), :].reshape(width, lanes)
            center = values - jnp.mean(values, axis=0, keepdims=True)
            spread = jnp.mean(center * center, axis=0, keepdims=True)
            normed = (
                center * lax.rsqrt(spread + 1e-05) * out_gain_ref[u] + out_bias_ref[u]
            ).astype(jnp.bfloat16)
            mixed = lax.dot_general(
                normed,
                out_w_ref[u],
                (((0,), (0,)), ((), ())),
                preferred_element_type=jnp.float32,
            )
            moved = gate_buf[u, ip] * mixed
            target[ip] = (source[ip].astype(jnp.float32) + moved[:side]).astype(jnp.bfloat16)
            target[ip + half] = (
                source[ip + half].astype(jnp.float32) + moved[side:]
            ).astype(jnp.bfloat16)

    def sums_of(u):
        for group in range(GROUPS):
            for part in range(PARTS):
                wait_edges(u, part, group)
            make_sums(u, group)
            for part in range(PARTS):
                send_sums(u, part, group)

    for part in range(PARTS):
        make_edges(0, part, pair_ref)
        if part == 0:
            pl.semaphore_wait(barrier, peers - 1)
        send_edges(0, part)
    sums_of(0)
    for part in range(PARTS):
        take_sums(0, part)
        mix(0, part, pair_ref, mid_ref)
        make_edges(1, part, mid_ref)
        send_edges(1, part)
    sums_of(1)
    for part in range(PARTS):
        take_sums(1, part)
        mix(1, part, mid_ref, out_ref)


def fused_on_device(rows, chan):
    def run(
        pair_act,
        pair_mask,
        input_gain,
        input_bias,
        proj_weight,
        gate_weight,
        output_gain,
        output_bias,
        out_weight,
    ):
        first, side, width = pair_act.shape
        half = first // 2
        hidden = proj_weight.shape[-1]
        peers = rows * chan
        owners = 2 * chan
        lanes = 2 * side
        block = (hidden // owners // GROUPS, half // PARTS, lanes)
        mask_float = pair_mask.astype(jnp.float32)
        mask_rows = jnp.concatenate([mask_float[:half], mask_float[half:]], axis=1)
        proj_flat = jnp.transpose(proj_weight, (0, 2, 3, 1)).reshape(2, 4 * hidden, width)
        vmem = pl.BlockSpec(memory_space=pltpu.VMEM)
        return pl.pallas_call(
            functools.partial(fused_kernel, rows, chan),
            out_shape=jax.ShapeDtypeStruct(pair_act.shape, jnp.bfloat16),
            in_specs=[vmem] * 9,
            out_specs=vmem,
            scratch_shapes=[
                pltpu.VMEM((first, side, width), jnp.bfloat16),
                pltpu.VMEM((hidden, half, lanes), jnp.float32),
                pltpu.VMEM((hidden, half, lanes), jnp.float32),
                pltpu.VMEM((hidden, half, lanes), jnp.float32),
                pltpu.VMEM((2, half, lanes, width), jnp.float32),
                pltpu.VMEM((2, PARTS, GROUPS, owners, *block), jnp.bfloat16),
                pltpu.VMEM((2, PARTS, GROUPS, owners, *block), jnp.bfloat16),
                pltpu.VMEM((2, PARTS, GROUPS, peers, *block), jnp.bfloat16),
                pltpu.VMEM((2, PARTS, GROUPS, owners, *block), jnp.bfloat16),
                pltpu.VMEM((2, PARTS, GROUPS, peers, *block), jnp.bfloat16),
                pltpu.VMEM((2, PARTS, GROUPS, peers, *block), jnp.bfloat16),
                *[pltpu.SemaphoreType.DMA((2, PARTS, GROUPS, peers))] * 6,
            ],
            compiler_params=pltpu.CompilerParams(
                collective_id=0, has_side_effects=True, vmem_limit_bytes=48 * 1024 * 1024
            ),
        )(
            pair_act,
            mask_rows,
            input_gain,
            input_bias,
            proj_flat,
            gate_weight,
            output_gain[:, :, None],
            output_bias[:, :, None],
            out_weight,
        )

    return run


def solution(mesh):
    in_specs = (
        P(("groups", "chan"), "rows", None),
        P(("groups", "chan"), "rows"),
        P(),
        P(),
        P(),
        P(),
        P(),
        P(),
        P(),
    )
    out_specs = P(("groups", "chan"), "rows", None)
    rows, chan = mesh.shape["rows"], mesh.shape["chan"]
    fused = fused_on_device(rows, chan)

    def choose(pair_act, pair_mask, *parameters):
        hidden = parameters[2].shape[-1]
        fits = (
            pair_act.shape[1] == 64
            and pair_act.shape[0] % (32 * PARTS) == 0
            and rows == 4
            and hidden % (2 * chan * GROUPS) == 0
        )
        body = fused if fits else on_device
        return body(pair_act, pair_mask, *parameters)

    return jax.shard_map(
        choose, mesh=mesh, in_specs=in_specs, out_specs=out_specs, check_vma=False
    )
```

```python
import functools

import jax
import jax.numpy as jnp
from jax import lax
from jax.experimental import pallas as pl
from jax.experimental.pallas import tpu as pltpu
from jax.sharding import PartitionSpec as P


def layer_norm(values, norm_gain, norm_bias):
    center = values - jnp.mean(values, axis=-1, keepdims=True)
    spread = jnp.mean(center * center, axis=-1, keepdims=True)
    return center * lax.rsqrt(spread + 1e-05) * norm_gain + norm_bias


def outgoing_sum(left_split, right_split):
    return jnp.einsum(
        "cik,cjk->cij",
        left_split,
        lax.all_gather(right_split, "chan", axis=1, tiled=True),
        preferred_element_type=jnp.float32,
    )


def incoming_sum(left_split, right_split):
    summed = lax.psum_scatter(
        jnp.einsum(
            "cki,ckj->icj", left_split, right_split, preferred_element_type=jnp.float32
        ).astype(jnp.bfloat16),
        "chan",
        scatter_dimension=0,
        tiled=True,
    ).astype(jnp.float32)
    return jnp.transpose(summed, (1, 0, 2))


def output_mix(combined, layer_index, output_gain, output_bias, out_weight):
    pixels = lax.all_to_all(combined, "rows", split_axis=2, concat_axis=0, tiled=True)
    values = pixels.astype(jnp.float32)
    center = values - jnp.mean(values, axis=0, keepdims=True)
    spread = jnp.mean(center * center, axis=0, keepdims=True)
    normed_out = (
        center * lax.rsqrt(spread + 1e-05) * output_gain[layer_index][:, None, None]
        + output_bias[layer_index][:, None, None]
    ).astype(jnp.bfloat16)
    return jnp.einsum(
        "cij,cd->ijd", normed_out, out_weight[layer_index], preferred_element_type=jnp.float32
    )


def tri_layer(
    pair_now,
    mask_float,
    layer_index,
    incoming,
    input_gain,
    input_bias,
    proj_weight,
    gate_weight,
    output_gain,
    output_bias,
    out_weight,
):
    normed_in = layer_norm(
        pair_now.astype(jnp.float32), input_gain[layer_index], input_bias[layer_index]
    ).astype(jnp.bfloat16)
    projected = jnp.einsum(
        "ijd,dhc->hcij", normed_in, proj_weight[layer_index], preferred_element_type=jnp.float32
    )
    left_edge = (jax.nn.sigmoid(projected[1]) * projected[0] * mask_float[None]).astype(
        jnp.bfloat16
    )
    right_edge = (jax.nn.sigmoid(projected[3]) * projected[2] * mask_float[None]).astype(
        jnp.bfloat16
    )
    gating = jax.nn.sigmoid(
        jnp.einsum(
            "ijd,de->ije", normed_in, gate_weight[layer_index], preferred_element_type=jnp.float32
        )
    )
    left_split, right_split = (
        lax.all_to_all(left_edge, "rows", split_axis=0, concat_axis=2, tiled=True),
        lax.all_to_all(right_edge, "rows", split_axis=0, concat_axis=2, tiled=True),
    )
    if incoming:
        combined = incoming_sum(left_split, right_split)
    else:
        combined = outgoing_sum(left_split, right_split)
    combined = lax.optimization_barrier(combined.astype(jnp.bfloat16))
    mixed_out = output_mix(combined, layer_index, output_gain, output_bias, out_weight)
    return lax.optimization_barrier(
        (pair_now.astype(jnp.float32) + gating * mixed_out).astype(jnp.bfloat16)
    )


def on_device(
    pair_act,
    pair_mask,
    input_gain,
    input_bias,
    proj_weight,
    gate_weight,
    output_gain,
    output_bias,
    out_weight,
):
    mask_float = pair_mask.astype(jnp.float32)
    after_out = tri_layer(
        pair_act,
        mask_float,
        0,
        False,
        input_gain,
        input_bias,
        proj_weight,
        gate_weight,
        output_gain,
        output_bias,
        out_weight,
    )
    return tri_layer(
        after_out,
        mask_float,
        1,
        True,
        input_gain,
        input_bias,
        proj_weight,
        gate_weight,
        output_gain,
        output_bias,
        out_weight,
    )


PARTS = 2
GROUPS = 2
UNROLL = 4


def sigmoid(values):
    return 0.5 * jnp.tanh(0.5 * values) + 0.5


def swap_halves(low, high):
    half = low.shape[-1] // 2
    lane = lax.broadcasted_iota(jnp.int32, low.shape, low.ndim - 1)
    axis = low.ndim - 1
    first = jnp.where(lane < half, low, pltpu.roll(high, half, axis))
    second = jnp.where(lane < half, pltpu.roll(low, half, axis), high)
    return first, second


def fused_kernel(
    rows,
    chan,
    pair_ref,
    mask_ref,
    in_gain_ref,
    in_bias_ref,
    proj_ref,
    gate_w_ref,
    out_gain_ref,
    out_bias_ref,
    out_w_ref,
    out_ref,
    mid_ref,
    left_wide,
    right_wide,
    sum_wide,
    gate_buf,
    normed_buf,
    mask_buf,
    column_buf,
    left_send,
    right_send,
    left_recv,
    right_recv,
    sum_send,
    sum_recv,
    left_ssem,
    left_rsem,
    right_ssem,
    right_rsem,
    sum_ssem,
    sum_rsem,
):
    owners = 2 * chan
    peers = rows * chan
    my_row = lax.axis_index("rows")
    my_chan = lax.axis_index("chan")
    my_half = lax.div(my_row, 2)
    slot = my_chan * 2 + lax.rem(my_row, 2)
    me = my_half * owners + slot
    side = pair_ref.shape[1]
    width = pair_ref.shape[2]
    half = pair_ref.shape[0] // 2
    batch = left_send.shape[4]
    depth = half // PARTS
    lanes = 2 * side

    def coords(peer):
        place = lax.rem(peer, owners)
        return {
            "rows": 2 * lax.div(peer, owners) + lax.rem(place, 2),
            "chan": lax.div(place, 2),
        }

    barrier = pltpu.get_barrier_semaphore()

    @pl.loop(1, peers)
    def _(step):
        peer = lax.rem(me + step, peers)
        pl.semaphore_signal(
            barrier, inc=1, device_id=coords(peer), device_id_type=pl.DeviceIdType.MESH
        )

    def near(step):
        return lax.rem(slot + step, owners)

    def remote(src, dst, ssem, rsem, peer):
        return pltpu.make_async_remote_copy(
            src_ref=src,
            dst_ref=dst,
            send_sem=ssem,
            recv_sem=rsem,
            device_id=coords(peer),
            device_id_type=pl.DeviceIdType.MESH,
        )

    def left_copy(u, part, group, step):
        where = (u, part, group)
        if u == 0:
            place, mine = near(step), slot
            peer = my_half * owners + place
        else:
            peer, mine = lax.rem(me + step, peers), me
            place = lax.rem(peer, owners)
        return remote(
            left_send.at[(*where, place)],
            left_recv.at[(*where, mine)],
            left_ssem.at[(*where, step)],
            left_rsem.at[(*where, step)],
            peer,
        )

    def right_copy(u, part, group, step):
        where = (u, part, group)
        return remote(
            right_send.at[(*where, near(step))],
            right_recv.at[(*where, slot)],
            right_ssem.at[(*where, step)],
            right_rsem.at[(*where, step)],
            my_half * owners + near(step),
        )

    def sum_copy(u, part, group, step):
        where = (u, part, group)
        if u == 0:
            place, mine = lax.rem(me + step, peers), me
            peer = place
        else:
            place, mine = near(step), slot
            peer = my_half * owners + place
        return remote(
            sum_send.at[(*where, place)],
            sum_recv.at[(*where, mine)],
            sum_ssem.at[(*where, step)],
            sum_rsem.at[(*where, step)],
            peer,
        )

    def norm_cells(u, part, source):
        @pl.loop(part * depth, (part + 1) * depth, unroll=UNROLL)
        def _(ip):
            cells = jnp.concatenate([source[ip], source[ip + half]], axis=0).astype(jnp.float32)
            center = cells - jnp.mean(cells, axis=-1, keepdims=True)
            spread = jnp.mean(center * center, axis=-1, keepdims=True)
            normed_buf[ip] = (
                center * lax.rsqrt(spread + 1e-05) * in_gain_ref[u : u + 1, :]
                + in_bias_ref[u : u + 1, :]
            ).astype(jnp.bfloat16)

    def make_gates(u):
        @pl.loop(0, half, unroll=UNROLL)
        def _(ip):
            gate_buf[ip] = sigmoid(
                jnp.dot(normed_buf[ip], gate_w_ref[u], preferred_element_type=jnp.float32)
            )

    def make_edges(u, part, group):
        count = width // GROUPS
        first = group * count

        @pl.loop(part * depth, (part + 1) * depth, unroll=UNROLL)
        def _(ip):
            projected = lax.dot_general(
                proj_ref[u, group],
                normed_buf[ip],
                (((1,), (1,)), ((), ())),
                preferred_element_type=jnp.float32,
            )
            mask_row = mask_buf[pl.ds(ip, 1), :]
            left = sigmoid(projected[count : 2 * count]) * projected[:count] * mask_row
            right = sigmoid(projected[3 * count :]) * projected[2 * count : 3 * count] * mask_row
            left_wide[first : first + count, pl.ds(ip, 1), :] = left[:, None, :]
            right_wide[first : first + count, pl.ds(ip, 1), :] = right[:, None, :]

    def send_edges(u, part, group):
        piece = slice(part * depth, (part + 1) * depth)

        @pl.loop(0, owners)
        def _(place):
            first = (group * owners + place) * batch
            left_send[u, part, group, place] = left_wide[pl.ds(first, batch), piece, :].astype(
                jnp.bfloat16
            )
            right_send[u, part, group, place] = right_wide[pl.ds(first, batch), piece, :].astype(
                jnp.bfloat16
            )

        @pl.loop(1, owners if u == 0 else peers)
        def _(step):
            left_copy(u, part, group, step).start()

        @pl.loop(1, owners)
        def _(step):
            right_copy(u, part, group, step).start()

        right_recv[u, part, group, slot] = right_send[u, part, group, slot]
        left_recv[u, part, group, slot if u == 0 else me] = left_send[u, part, group, slot]

    def wait_edges(u, part, group):
        @pl.loop(1, owners)
        def _(step):
            right_copy(u, part, group, step).wait()

        @pl.loop(1, owners if u == 0 else peers)
        def _(step):
            left_copy(u, part, group, step).wait()

    def make_sums(u, group):
        @pl.loop(0, batch, unroll=2)
        def _(c):
            def whole(edges, first):
                pieces = []
                for a in range(chan):
                    low, high = (
                        jnp.concatenate(
                            [edges[u, part, group, place, c] for part in range(PARTS)], axis=0
                        ).astype(jnp.float32)
                        for place in (first + 2 * a, first + 2 * a + 1)
                    )
                    pieces.extend(swap_halves(low, high))
                return jnp.concatenate(pieces, axis=0).astype(jnp.bfloat16)

            if u == 0:
                left = whole(left_recv, 0)
            else:
                left = jnp.concatenate([whole(left_recv, 0), whole(left_recv, owners)], axis=1)
            right = whole(right_recv, 0)
            over = 1 if u == 0 else 0
            summed = lax.dot_general(
                left,
                right,
                (((over,), (over,)), ((), ())),
                preferred_element_type=jnp.float32,
            )
            for a in range(chan):
                for tile in range(summed.shape[1] // lanes):
                    top = 2 * half * a
                    columns = slice(tile * lanes, (tile + 1) * lanes)
                    one, two = swap_halves(
                        summed[top : top + half, columns],
                        summed[top + half : top + 2 * half, columns],
                    )
                    place = tile * owners + 2 * a
                    for part in range(PARTS):
                        piece = slice(part * depth, (part + 1) * depth)
                        sum_send[u, part, group, place, c] = one[piece].astype(jnp.bfloat16)
                        sum_send[u, part, group, place + 1, c] = two[piece].astype(jnp.bfloat16)

    def send_sums(u, part, group):
        @pl.loop(1, peers if u == 0 else owners)
        def _(step):
            sum_copy(u, part, group, step).start()

    def take_sums(u, part):
        piece = slice(part * depth, (part + 1) * depth)
        mine = me if u == 0 else slot
        for group in range(GROUPS):
            sum_recv[u, part, group, mine] = sum_send[u, part, group, mine]

            @pl.loop(1, peers if u == 0 else owners)
            def _(step):
                sum_copy(u, part, group, step).wait()

            @pl.loop(0, owners)
            def _(place):
                total = sum_recv[u, part, group, place].astype(jnp.float32)
                if u == 0:
                    total += sum_recv[u, part, group, place + owners].astype(jnp.float32)
                first = (group * owners + place) * batch
                sum_wide[pl.ds(first, batch), piece, :] = total

    def mix(u, part, source, target):
        @pl.loop(part * depth, (part + 1) * depth, unroll=UNROLL)
        def _(ip):
            values = sum_wide[:, pl.ds(ip, 1), :].reshape(width, lanes)
            center = values - jnp.mean(values, axis=0, keepdims=True)
            spread = jnp.mean(center * center, axis=0, keepdims=True)
            normed = (
                center * lax.rsqrt(spread + 1e-05) * column_buf[0, u] + column_buf[1, u]
            ).astype(jnp.bfloat16)
            mixed = lax.dot_general(
                normed,
                out_w_ref[u],
                (((0,), (0,)), ((), ())),
                preferred_element_type=jnp.float32,
            )
            moved = gate_buf[ip] * mixed
            target[ip] = (source[ip].astype(jnp.float32) + moved[:side]).astype(jnp.bfloat16)
            target[ip + half] = (
                source[ip + half].astype(jnp.float32) + moved[side:]
            ).astype(jnp.bfloat16)

    def sums_of(u):
        for group in range(GROUPS):
            for part in range(PARTS):
                wait_edges(u, part, group)
            make_sums(u, group)
            for part in range(PARTS):
                send_sums(u, part, group)

    mask_buf[:, :side] = mask_ref[:half].astype(jnp.float32)
    mask_buf[:, side:] = mask_ref[half:].astype(jnp.float32)
    for group in range(GROUPS):
        for part in range(PARTS):
            if group == 0:
                norm_cells(0, part, pair_ref)
            make_edges(0, part, group)
            if group == 0 and part == 0:
                pl.semaphore_wait(barrier, peers - 1)
            send_edges(0, part, group)
    for index, vector in enumerate((out_gain_ref, out_bias_ref)):
        for u in range(2):
            column_buf[index, u] = jnp.transpose(
                jnp.broadcast_to(vector[u : u + 1, :], (lanes, width))
            )
    make_gates(0)
    sums_of(0)
    for part in range(PARTS):
        take_sums(0, part)
        mix(0, part, pair_ref, mid_ref)
        norm_cells(1, part, mid_ref)
        for group in range(GROUPS):
            make_edges(1, part, group)
            send_edges(1, part, group)
    make_gates(1)
    sums_of(1)
    for part in range(PARTS):
        take_sums(1, part)
        mix(1, part, mid_ref, out_ref)


def fused_on_device(rows, chan):
    def run(
        pair_act,
        pair_mask,
        input_gain,
        input_bias,
        proj_weight,
        gate_weight,
        output_gain,
        output_bias,
        out_weight,
    ):
        first, side, width = pair_act.shape
        half = first // 2
        hidden = proj_weight.shape[-1]
        peers = rows * chan
        owners = 2 * chan
        lanes = 2 * side
        block = (hidden // owners // GROUPS, half // PARTS, lanes)
        grouped = proj_weight.reshape(2, width, 4, GROUPS, hidden // GROUPS)
        proj_flat = jnp.transpose(grouped, (0, 3, 2, 4, 1)).reshape(
            2, GROUPS, 4 * hidden // GROUPS, width
        )
        vmem = pl.BlockSpec(memory_space=pltpu.VMEM)
        return pl.pallas_call(
            functools.partial(fused_kernel, rows, chan),
            out_shape=jax.ShapeDtypeStruct(pair_act.shape, jnp.bfloat16),
            in_specs=[vmem] * 9,
            out_specs=vmem,
            scratch_shapes=[
                pltpu.VMEM((first, side, width), jnp.bfloat16),
                pltpu.VMEM((hidden, half, lanes), jnp.float32),
                pltpu.VMEM((hidden, half, lanes), jnp.float32),
                pltpu.VMEM((hidden, half, lanes), jnp.float32),
                pltpu.VMEM((half, lanes, width), jnp.float32),
                pltpu.VMEM((half, lanes, width), jnp.bfloat16),
                pltpu.VMEM((half, lanes), jnp.float32),
                pltpu.VMEM((2, 2, hidden, lanes), jnp.float32),
                pltpu.VMEM((2, PARTS, GROUPS, owners, *block), jnp.bfloat16),
                pltpu.VMEM((2, PARTS, GROUPS, owners, *block), jnp.bfloat16),
                pltpu.VMEM((2, PARTS, GROUPS, peers, *block), jnp.bfloat16),
                pltpu.VMEM((2, PARTS, GROUPS, owners, *block), jnp.bfloat16),
                pltpu.VMEM((2, PARTS, GROUPS, peers, *block), jnp.bfloat16),
                pltpu.VMEM((2, PARTS, GROUPS, peers, *block), jnp.bfloat16),
                *[pltpu.SemaphoreType.DMA((2, PARTS, GROUPS, peers))] * 6,
            ],
            compiler_params=pltpu.CompilerParams(
                collective_id=0, has_side_effects=True, vmem_limit_bytes=48 * 1024 * 1024
            ),
        )(
            pair_act,
            pair_mask,
            input_gain,
            input_bias,
            proj_flat,
            gate_weight,
            output_gain,
            output_bias,
            out_weight,
        )

    return run


def solution(mesh):
    in_specs = (
        P(("groups", "chan"), "rows", None),
        P(("groups", "chan"), "rows"),
        P(),
        P(),
        P(),
        P(),
        P(),
        P(),
        P(),
    )
    out_specs = P(("groups", "chan"), "rows", None)
    rows, chan = mesh.shape["rows"], mesh.shape["chan"]
    fused = fused_on_device(rows, chan)

    def choose(pair_act, pair_mask, *parameters):
        hidden = parameters[2].shape[-1]
        fits = (
            pair_act.shape[1] == 64
            and pair_act.shape[0] % (32 * PARTS) == 0
            and rows == 4
            and hidden % (2 * chan * GROUPS) == 0
        )
        body = fused if fits else on_device
        return body(pair_act, pair_mask, *parameters)

    return jax.shard_map(
        choose, mesh=mesh, in_specs=in_specs, out_specs=out_specs, check_vma=False
    )
```

```python
import functools

import jax
import jax.numpy as jnp
from jax import lax
from jax.experimental import pallas as pl
from jax.experimental.pallas import tpu as pltpu
from jax.sharding import PartitionSpec as P


def layer_norm(values, norm_gain, norm_bias):
    center = values - jnp.mean(values, axis=-1, keepdims=True)
    spread = jnp.mean(center * center, axis=-1, keepdims=True)
    return center * lax.rsqrt(spread + 1e-05) * norm_gain + norm_bias


def outgoing_sum(left_split, right_split):
    return jnp.einsum(
        "cik,cjk->cij",
        left_split,
        lax.all_gather(right_split, "chan", axis=1, tiled=True),
        preferred_element_type=jnp.float32,
    )


def incoming_sum(left_split, right_split):
    summed = lax.psum_scatter(
        jnp.einsum(
            "cki,ckj->icj", left_split, right_split, preferred_element_type=jnp.float32
        ).astype(jnp.bfloat16),
        "chan",
        scatter_dimension=0,
        tiled=True,
    ).astype(jnp.float32)
    return jnp.transpose(summed, (1, 0, 2))


def output_mix(combined, layer_index, output_gain, output_bias, out_weight):
    pixels = lax.all_to_all(combined, "rows", split_axis=2, concat_axis=0, tiled=True)
    values = pixels.astype(jnp.float32)
    center = values - jnp.mean(values, axis=0, keepdims=True)
    spread = jnp.mean(center * center, axis=0, keepdims=True)
    normed_out = (
        center * lax.rsqrt(spread + 1e-05) * output_gain[layer_index][:, None, None]
        + output_bias[layer_index][:, None, None]
    ).astype(jnp.bfloat16)
    return jnp.einsum(
        "cij,cd->ijd", normed_out, out_weight[layer_index], preferred_element_type=jnp.float32
    )


def tri_layer(
    pair_now,
    mask_float,
    layer_index,
    incoming,
    input_gain,
    input_bias,
    proj_weight,
    gate_weight,
    output_gain,
    output_bias,
    out_weight,
):
    normed_in = layer_norm(
        pair_now.astype(jnp.float32), input_gain[layer_index], input_bias[layer_index]
    ).astype(jnp.bfloat16)
    projected = jnp.einsum(
        "ijd,dhc->hcij", normed_in, proj_weight[layer_index], preferred_element_type=jnp.float32
    )
    left_edge = (jax.nn.sigmoid(projected[1]) * projected[0] * mask_float[None]).astype(
        jnp.bfloat16
    )
    right_edge = (jax.nn.sigmoid(projected[3]) * projected[2] * mask_float[None]).astype(
        jnp.bfloat16
    )
    gating = jax.nn.sigmoid(
        jnp.einsum(
            "ijd,de->ije", normed_in, gate_weight[layer_index], preferred_element_type=jnp.float32
        )
    )
    left_split, right_split = (
        lax.all_to_all(left_edge, "rows", split_axis=0, concat_axis=2, tiled=True),
        lax.all_to_all(right_edge, "rows", split_axis=0, concat_axis=2, tiled=True),
    )
    if incoming:
        combined = incoming_sum(left_split, right_split)
    else:
        combined = outgoing_sum(left_split, right_split)
    combined = lax.optimization_barrier(combined.astype(jnp.bfloat16))
    mixed_out = output_mix(combined, layer_index, output_gain, output_bias, out_weight)
    return lax.optimization_barrier(
        (pair_now.astype(jnp.float32) + gating * mixed_out).astype(jnp.bfloat16)
    )


def on_device(
    pair_act,
    pair_mask,
    input_gain,
    input_bias,
    proj_weight,
    gate_weight,
    output_gain,
    output_bias,
    out_weight,
):
    mask_float = pair_mask.astype(jnp.float32)
    after_out = tri_layer(
        pair_act,
        mask_float,
        0,
        False,
        input_gain,
        input_bias,
        proj_weight,
        gate_weight,
        output_gain,
        output_bias,
        out_weight,
    )
    return tri_layer(
        after_out,
        mask_float,
        1,
        True,
        input_gain,
        input_bias,
        proj_weight,
        gate_weight,
        output_gain,
        output_bias,
        out_weight,
    )


PARTS = 2
GROUPS = 2
UNROLL = 8


def sigmoid(values):
    return 0.5 * jnp.tanh(0.5 * values) + 0.5


def swap_halves(low, high):
    half = low.shape[-1] // 2
    lane = lax.broadcasted_iota(jnp.int32, low.shape, low.ndim - 1)
    axis = low.ndim - 1
    first = jnp.where(lane < half, low, pltpu.roll(high, half, axis))
    second = jnp.where(lane < half, pltpu.roll(low, half, axis), high)
    return first, second


def fused_kernel(
    rows,
    chan,
    pair_ref,
    mask_ref,
    in_gain_ref,
    in_bias_ref,
    proj_ref,
    gate_w_ref,
    out_gain_ref,
    out_bias_ref,
    out_w_ref,
    out_ref,
    mid_ref,
    left_wide,
    right_wide,
    sum_wide,
    gate_buf,
    normed_buf,
    mask_buf,
    column_buf,
    left_send,
    right_send,
    left_recv,
    right_recv,
    sum_send,
    sum_recv,
    left_ssem,
    left_rsem,
    right_ssem,
    right_rsem,
    sum_ssem,
    sum_rsem,
):
    owners = 2 * chan
    peers = rows * chan
    my_row = lax.axis_index("rows")
    my_chan = lax.axis_index("chan")
    my_half = lax.div(my_row, 2)
    slot = my_chan * 2 + lax.rem(my_row, 2)
    me = my_half * owners + slot
    side = pair_ref.shape[1]
    width = pair_ref.shape[2]
    half = pair_ref.shape[0] // 2
    batch = left_send.shape[4]
    depth = half // PARTS
    lanes = 2 * side

    def coords(peer):
        place = lax.rem(peer, owners)
        return {
            "rows": 2 * lax.div(peer, owners) + lax.rem(place, 2),
            "chan": lax.div(place, 2),
        }

    barrier = pltpu.get_barrier_semaphore()

    @pl.loop(1, peers)
    def _(step):
        peer = lax.rem(me + step, peers)
        pl.semaphore_signal(
            barrier, inc=1, device_id=coords(peer), device_id_type=pl.DeviceIdType.MESH
        )

    def near(step):
        return lax.rem(slot + step, owners)

    def remote(src, dst, ssem, rsem, peer):
        return pltpu.make_async_remote_copy(
            src_ref=src,
            dst_ref=dst,
            send_sem=ssem,
            recv_sem=rsem,
            device_id=coords(peer),
            device_id_type=pl.DeviceIdType.MESH,
        )

    def left_copy(u, part, group, step):
        where = (u, part, group)
        if u == 0:
            place, mine = near(step), slot
            peer = my_half * owners + place
        else:
            peer, mine = lax.rem(me + step, peers), me
            place = lax.rem(peer, owners)
        return remote(
            left_send.at[(*where, place)],
            left_recv.at[(*where, mine)],
            left_ssem.at[(*where, step)],
            left_rsem.at[(*where, step)],
            peer,
        )

    def right_copy(u, part, group, step):
        where = (u, part, group)
        return remote(
            right_send.at[(*where, near(step))],
            right_recv.at[(*where, slot)],
            right_ssem.at[(*where, step)],
            right_rsem.at[(*where, step)],
            my_half * owners + near(step),
        )

    def sum_copy(u, part, group, step):
        where = (u, part, group)
        if u == 0:
            place, mine = lax.rem(me + step, peers), me
            peer = place
        else:
            place, mine = near(step), slot
            peer = my_half * owners + place
        return remote(
            sum_send.at[(*where, place)],
            sum_recv.at[(*where, mine)],
            sum_ssem.at[(*where, step)],
            sum_rsem.at[(*where, step)],
            peer,
        )

    def norm_cells(u, part, source):
        @pl.loop(part * depth, (part + 1) * depth, unroll=UNROLL)
        def _(ip):
            cells = jnp.concatenate([source[ip], source[ip + half]], axis=0).astype(jnp.float32)
            center = cells - jnp.mean(cells, axis=-1, keepdims=True)
            spread = jnp.mean(center * center, axis=-1, keepdims=True)
            normed_buf[ip] = (
                center * lax.rsqrt(spread + 1e-05) * in_gain_ref[u : u + 1, :]
                + in_bias_ref[u : u + 1, :]
            ).astype(jnp.bfloat16)

    def make_gates(u):
        @pl.loop(0, half, unroll=UNROLL)
        def _(ip):
            gate_buf[ip] = sigmoid(
                jnp.dot(normed_buf[ip], gate_w_ref[u], preferred_element_type=jnp.float32)
            )

    def make_edges(u, part, group):
        count = width // GROUPS
        first = group * count

        @pl.loop(part * depth, (part + 1) * depth, unroll=UNROLL)
        def _(ip):
            projected = lax.dot_general(
                proj_ref[u, group],
                normed_buf[ip],
                (((1,), (1,)), ((), ())),
                preferred_element_type=jnp.float32,
            )
            mask_row = mask_buf[pl.ds(ip, 1), :]
            left = sigmoid(projected[count : 2 * count]) * projected[:count] * mask_row
            right = sigmoid(projected[3 * count :]) * projected[2 * count : 3 * count] * mask_row
            left_wide[first : first + count, pl.ds(ip, 1), :] = left[:, None, :]
            right_wide[first : first + count, pl.ds(ip, 1), :] = right[:, None, :]

    def send_edges(u, part, group):
        piece = slice(part * depth, (part + 1) * depth)

        @pl.loop(0, owners)
        def _(place):
            first = (group * owners + place) * batch
            left_send[u, part, group, place] = left_wide[pl.ds(first, batch), piece, :].astype(
                jnp.bfloat16
            )
            right_send[u, part, group, place] = right_wide[pl.ds(first, batch), piece, :].astype(
                jnp.bfloat16
            )

        @pl.loop(1, owners if u == 0 else peers)
        def _(step):
            left_copy(u, part, group, step).start()

        @pl.loop(1, owners)
        def _(step):
            right_copy(u, part, group, step).start()

        right_recv[u, part, group, slot] = right_send[u, part, group, slot]
        left_recv[u, part, group, slot if u == 0 else me] = left_send[u, part, group, slot]

    def wait_edges(u, part, group):
        @pl.loop(1, owners)
        def _(step):
            right_copy(u, part, group, step).wait()

        @pl.loop(1, owners if u == 0 else peers)
        def _(step):
            left_copy(u, part, group, step).wait()

    def make_sums(u, group):
        @pl.loop(0, batch, unroll=2)
        def _(c):
            def whole(edges, first):
                pieces = []
                for a in range(chan):
                    low, high = (
                        jnp.concatenate(
                            [edges[u, part, group, place, c] for part in range(PARTS)], axis=0
                        ).astype(jnp.float32)
                        for place in (first + 2 * a, first + 2 * a + 1)
                    )
                    pieces.extend(swap_halves(low, high))
                return jnp.concatenate(pieces, axis=0).astype(jnp.bfloat16)

            if u == 0:
                left = whole(left_recv, 0)
            else:
                left = jnp.concatenate([whole(left_recv, 0), whole(left_recv, owners)], axis=1)
            right = whole(right_recv, 0)
            over = 1 if u == 0 else 0
            summed = lax.dot_general(
                left,
                right,
                (((over,), (over,)), ((), ())),
                preferred_element_type=jnp.float32,
            )
            for a in range(chan):
                for tile in range(summed.shape[1] // lanes):
                    top = 2 * half * a
                    columns = slice(tile * lanes, (tile + 1) * lanes)
                    one, two = swap_halves(
                        summed[top : top + half, columns],
                        summed[top + half : top + 2 * half, columns],
                    )
                    place = tile * owners + 2 * a
                    for part in range(PARTS):
                        piece = slice(part * depth, (part + 1) * depth)
                        sum_send[u, part, group, place, c] = one[piece].astype(jnp.bfloat16)
                        sum_send[u, part, group, place + 1, c] = two[piece].astype(jnp.bfloat16)

    def send_sums(u, part, group):
        @pl.loop(1, peers if u == 0 else owners)
        def _(step):
            sum_copy(u, part, group, step).start()

    def take_sums(u, part):
        piece = slice(part * depth, (part + 1) * depth)
        mine = me if u == 0 else slot
        for group in range(GROUPS):
            sum_recv[u, part, group, mine] = sum_send[u, part, group, mine]

            @pl.loop(1, peers if u == 0 else owners)
            def _(step):
                sum_copy(u, part, group, step).wait()

            @pl.loop(0, owners)
            def _(place):
                total = sum_recv[u, part, group, place].astype(jnp.float32)
                if u == 0:
                    total += sum_recv[u, part, group, place + owners].astype(jnp.float32)
                first = (group * owners + place) * batch
                sum_wide[pl.ds(first, batch), piece, :] = total

    def mix(u, part, source, target):
        @pl.loop(part * depth, (part + 1) * depth, unroll=UNROLL)
        def _(ip):
            values = sum_wide[:, pl.ds(ip, 1), :].reshape(width, lanes)
            center = values - jnp.mean(values, axis=0, keepdims=True)
            spread = jnp.mean(center * center, axis=0, keepdims=True)
            normed = (
                center * lax.rsqrt(spread + 1e-05) * column_buf[0, u] + column_buf[1, u]
            ).astype(jnp.bfloat16)
            mixed = lax.dot_general(
                normed,
                out_w_ref[u],
                (((0,), (0,)), ((), ())),
                preferred_element_type=jnp.float32,
            )
            moved = gate_buf[ip] * mixed
            target[ip] = (source[ip].astype(jnp.float32) + moved[:side]).astype(jnp.bfloat16)
            target[ip + half] = (
                source[ip + half].astype(jnp.float32) + moved[side:]
            ).astype(jnp.bfloat16)

    def sums_of(u):
        for group in range(GROUPS):
            for part in range(PARTS):
                wait_edges(u, part, group)
            make_sums(u, group)
            for part in range(PARTS):
                send_sums(u, part, group)

    mask_buf[:, :side] = mask_ref[:half].astype(jnp.float32)
    mask_buf[:, side:] = mask_ref[half:].astype(jnp.float32)
    for group in range(GROUPS):
        for part in range(PARTS):
            if group == 0:
                norm_cells(0, part, pair_ref)
            make_edges(0, part, group)
            if group == 0 and part == 0:
                pl.semaphore_wait(barrier, peers - 1)
            send_edges(0, part, group)
    for index, vector in enumerate((out_gain_ref, out_bias_ref)):
        for u in range(2):
            column_buf[index, u] = jnp.transpose(
                jnp.broadcast_to(vector[u : u + 1, :], (lanes, width))
            )
    make_gates(0)
    sums_of(0)
    for part in range(PARTS):
        take_sums(0, part)
        mix(0, part, pair_ref, mid_ref)
        norm_cells(1, part, mid_ref)
        for group in range(GROUPS):
            make_edges(1, part, group)
            send_edges(1, part, group)
    make_gates(1)
    sums_of(1)
    for part in range(PARTS):
        take_sums(1, part)
        mix(1, part, mid_ref, out_ref)


def fused_on_device(rows, chan):
    def run(
        pair_act,
        pair_mask,
        input_gain,
        input_bias,
        proj_weight,
        gate_weight,
        output_gain,
        output_bias,
        out_weight,
    ):
        first, side, width = pair_act.shape
        half = first // 2
        hidden = proj_weight.shape[-1]
        peers = rows * chan
        owners = 2 * chan
        lanes = 2 * side
        block = (hidden // owners // GROUPS, half // PARTS, lanes)
        grouped = proj_weight.reshape(2, width, 4, GROUPS, hidden // GROUPS)
        proj_flat = jnp.transpose(grouped, (0, 3, 2, 4, 1)).reshape(
            2, GROUPS, 4 * hidden // GROUPS, width
        )
        vmem = pl.BlockSpec(memory_space=pltpu.VMEM)
        return pl.pallas_call(
            functools.partial(fused_kernel, rows, chan),
            out_shape=jax.ShapeDtypeStruct(pair_act.shape, jnp.bfloat16),
            in_specs=[vmem] * 9,
            out_specs=vmem,
            scratch_shapes=[
                pltpu.VMEM((first, side, width), jnp.bfloat16),
                pltpu.VMEM((hidden, half, lanes), jnp.float32),
                pltpu.VMEM((hidden, half, lanes), jnp.float32),
                pltpu.VMEM((hidden, half, lanes), jnp.float32),
                pltpu.VMEM((half, lanes, width), jnp.float32),
                pltpu.VMEM((half, lanes, width), jnp.bfloat16),
                pltpu.VMEM((half, lanes), jnp.float32),
                pltpu.VMEM((2, 2, hidden, lanes), jnp.float32),
                pltpu.VMEM((2, PARTS, GROUPS, owners, *block), jnp.bfloat16),
                pltpu.VMEM((2, PARTS, GROUPS, owners, *block), jnp.bfloat16),
                pltpu.VMEM((2, PARTS, GROUPS, peers, *block), jnp.bfloat16),
                pltpu.VMEM((2, PARTS, GROUPS, owners, *block), jnp.bfloat16),
                pltpu.VMEM((2, PARTS, GROUPS, peers, *block), jnp.bfloat16),
                pltpu.VMEM((2, PARTS, GROUPS, peers, *block), jnp.bfloat16),
                *[pltpu.SemaphoreType.DMA((2, PARTS, GROUPS, peers))] * 6,
            ],
            compiler_params=pltpu.CompilerParams(
                collective_id=0, has_side_effects=True, vmem_limit_bytes=48 * 1024 * 1024
            ),
        )(
            pair_act,
            pair_mask,
            input_gain,
            input_bias,
            proj_flat,
            gate_weight,
            output_gain,
            output_bias,
            out_weight,
        )

    return run


def solution(mesh):
    in_specs = (
        P(("groups", "chan"), "rows", None),
        P(("groups", "chan"), "rows"),
        P(),
        P(),
        P(),
        P(),
        P(),
        P(),
        P(),
    )
    out_specs = P(("groups", "chan"), "rows", None)
    rows, chan = mesh.shape["rows"], mesh.shape["chan"]
    fused = fused_on_device(rows, chan)

    def choose(pair_act, pair_mask, *parameters):
        hidden = parameters[2].shape[-1]
        fits = (
            pair_act.shape[1] == 64
            and pair_act.shape[0] % (32 * PARTS) == 0
            and rows == 4
            and hidden % (2 * chan * GROUPS) == 0
        )
        body = fused if fits else on_device
        return body(pair_act, pair_mask, *parameters)

    return jax.shard_map(
        choose, mesh=mesh, in_specs=in_specs, out_specs=out_specs, check_vma=False
    )
```
